32 devices in a mesh: ctx: 8 (over y, x, core), sp: 4 (over z).
Axes of the slice: x: 2, y: 2, z: 4, core: 2. Of those that a mesh axis runs over, the one named last changes fastest.
Arguments:
- layer_input: bfloat16 [4096, 2560], P(('ctx', 'sp')), may hold values from -6 to 6
- proj_weight: bfloat16 [2560, 5120], P('ctx', 'sp'), may hold values from -0.125 to 0.125
- state_weight: bfloat16 [2560, 256], replicated, may hold values from -0.125 to 0.125
- out_grad: bfloat16 [4096, 5120], P('ctx', 'sp'), may hold values from -6 to 6
- log_decay: float32 [80, 4096], P('sp', 'ctx'), may hold values from -1 to 0, as said below
- skip_gain: float32 [80], P('sp'), may hold values from 0.5 to 1.5
Outputs:
- grad_input: bfloat16 [4096, 2560], P(('ctx', 'sp'))
- grad_proj: float32 [2560, 5120], P('ctx', 'sp')
- grad_state: float32 [2560, 256], P(('ctx', 'sp'))
The draws below stay inside these ranges and needn't reach their ends.
Inputs may be any that keep to these rules, and one draw needn't show every extreme that they name: `log_decay`: every entry is below zero.
All inputs are finite; a program needn't handle non-finite values.
Results may differ from the reference program's by a relative error of at most 0.025.
Values may be sent and summed in bfloat16 or wider, within the bound.
A program may use at most 128 MiB of HBM per device.

```python
import math
import jax
import jax.numpy as jnp
from jax import lax

D = 2560
H = 80
P_SIZE = 64
N = 128
BLOCK = 256
SEQUENCE_TOKENS = 4096


def draw_log_decay(key, part):
    key = jax.random.fold_in(key, 7)
    subkeys = jax.random.split(key, 6)
    slow_share = 0.5
    slow_head = jax.random.uniform(subkeys[0], (H, 1), jnp.float32) < slow_share
    slow_rate = jnp.exp(jax.random.uniform(subkeys[1], (H, 1), jnp.float32, math.log(0.2), math.log(0.6))) / SEQUENCE_TOKENS
    fast_rate = jnp.exp(jax.random.uniform(subkeys[2], (H, 1), jnp.float32, math.log(1.0 / 50.0), math.log(1.0 / 30.0)))
    roughness = jnp.exp(jax.random.uniform(subkeys[3], (H, SEQUENCE_TOKENS), jnp.float32, math.log(0.5), math.log(2.0)))
    steady_level = -jnp.where(slow_head, slow_rate, fast_rate) * roughness
    token_positions = jax.random.randint(subkeys[4], (H, 2), 0, SEQUENCE_TOKENS)
    spike_mask = jnp.any(jnp.arange(SEQUENCE_TOKENS)[None, None, :] == token_positions[:, :, None], axis=1)
    decay_strength = jnp.log(jax.random.uniform(subkeys[5], (H, SEQUENCE_TOKENS), jnp.float32, 0.5, 0.8))
    return jnp.where(spike_mask, decay_strength, steady_level).astype(jnp.float32)


def spiked(drawn, rng, source, target, shards_of, factor):
    owner, partner = [(jnp.arange(drawn.shape[position]) // (drawn.shape[position] // shards_of)).reshape([-1 if axis == position else 1 for axis in range(drawn.ndim)]) for position in (source, target)]
    chosen = jax.random.permutation(rng, shards_of)[partner]
    strong = (owner == chosen) | (owner == (partner + shards_of // 2) % shards_of)
    return jnp.where(strong, factor * drawn, drawn)


def levels(own_key, shape, cuts, low, top_value):
    factor_of, own = 1.0, jax.random.fold_in(own_key, 6)
    for dim, shards_of in cuts:
        draws = jnp.exp(jax.random.uniform(jax.random.fold_in(own, dim), (shards_of,), jnp.float32, low / len(cuts), top_value / len(cuts)))
        factor_of = factor_of * jnp.repeat(draws, shape[dim] // shards_of).reshape([-1 if axis == dim else 1 for axis in range(len(shape))])
    return factor_of


def bell_draw(rng, shape, width, bound, cuts=(), held_as=jnp.bfloat16):
    drawn = jax.random.normal(rng, shape, jnp.float32) * width
    if len(cuts) > 0:
        drawn = levels(rng, shape, cuts, -0.22, 0.18) * drawn
    return jnp.clip(drawn, min=-bound, max=bound).astype(held_as)


def heavy_noise(key, shape, width, limit, cuts, heavy, kind=jnp.bfloat16):
    entries = width * jax.random.normal(key, shape, jnp.float32)
    if cuts:
        entries = entries * levels(key, shape, cuts, -0.22, 0.18)
    return jnp.clip(spiked(entries, jax.random.fold_in(key, 3), *heavy), -limit, limit).astype(kind)


def setup_inputs(seed: int = 0) -> dict:
    streams_of = jax.random.split(jax.random.key(seed), 7)
    return {
        "layer_input": heavy_noise(streams_of[0], (SEQUENCE_TOKENS, D), 1.0, 6.0, ((0, 32),), (0, 1, 32, 2.75)),
        "proj_weight": bell_draw(streams_of[1], (D, H * P_SIZE), D ** -0.5, 0.125, ((0, 8), (1, 4))),
        "state_weight": bell_draw(streams_of[2], (D, 2 * N), D ** -0.5, 0.125),
        "out_grad": bell_draw(streams_of[3], (SEQUENCE_TOKENS, H * P_SIZE), 1.0, 6.0, ((0, 8), (1, 4))),
        "log_decay": draw_log_decay(jax.random.fold_in(streams_of[6], 71), 0),
        "skip_gain": jnp.clip(0.5 + 1.0 * jax.random.uniform(streams_of[5], (H,), jnp.float32) ** levels(streams_of[5], (H,), ((0, 4),), -0.2, 0.2), 0.5, 1.5),
    }


exact_precision = lax.Precision.HIGHEST

def contract(form, left, right):
    return jnp.einsum(form, left.astype(jnp.float32), right.astype(jnp.float32), precision=exact_precision)

def combine(preceding_tokens, later):
    leading_decay, first_state = preceding_tokens
    last_decay, last_state = later
    return (leading_decay * last_decay, last_decay[:, None, None] * first_state + last_state)

def forward_step(carried, element):
    return (combine(carried, element), carried)

def split_heads(matrix, count_of_heads):
    row_total, col_total = matrix.shape
    block_count = row_total // BLOCK
    shaped = matrix.reshape(block_count, BLOCK, count_of_heads, col_total // count_of_heads)
    return shaped.transpose(0, 2, 1, 3)

def merge_heads(grads):
    block_count, count_of_heads, length, head_width = grads.shape
    return grads.transpose(0, 2, 1, 3).reshape(block_count * length, count_of_heads * head_width)

def decay_blocks(log_decay):
    count_of_heads, row_total = log_decay.shape
    shaped = log_decay.reshape(count_of_heads, row_total // BLOCK, BLOCK)
    cumulative = jnp.cumsum(shaped, axis=2).transpose(1, 0, 2)
    input_gate = jnp.sqrt(-jnp.expm1(2.0 * shaped)).transpose(1, 0, 2)
    return (cumulative, input_gate)

def weighted_inputs(values, cotangent, cumulative, input_gate):
    to_end = jnp.exp(cumulative[:, -1:] - cumulative)
    gated_values = (values * (input_gate * to_end)[:, :, None]).astype(jnp.bfloat16)
    scaled_cot = (cotangent * jnp.exp(cumulative)[:, :, None]).astype(jnp.bfloat16)
    return (gated_values, scaled_cot)

def block_summary(values, cotangent, writer, reader, cumulative, input_gate):
    norm_scale = writer.shape[1] ** (-0.5)
    gated_values, scaled_cot = weighted_inputs(values, cotangent, cumulative, input_gate)
    written = contract('sn,hsp->hnp', writer, gated_values)
    pending = contract('sn,hsp->hnp', reader, scaled_cot) * norm_scale
    return (jnp.exp(cumulative[:, -1]), written, pending)

def block_grads(values, cotangent, writer, reader, cumulative, input_gate, state_in, adjoint_in, skip_gain):
    norm_scale = writer.shape[1] ** (-0.5)
    length = cumulative.shape[1]
    causal = (jnp.arange(length)[:, None] >= jnp.arange(length)[None, :])[None]
    exponent = cumulative[:, :, None] - cumulative[:, None, :]
    decays = jnp.where(causal, jnp.exp(jnp.where(causal, exponent, 0.0)), 0.0)
    to_end = jnp.exp(cumulative[:, -1:] - cumulative)
    gated_values, scaled_cot = weighted_inputs(values, cotangent, cumulative, input_gate)
    state_low = state_in.astype(jnp.bfloat16)
    adjoint_low = adjoint_in.astype(jnp.bfloat16)
    gram_grad = contract('htp,hsp->hts', cotangent, values)
    weighted = (decays * gram_grad * input_gate[:, None, :]).astype(jnp.bfloat16)
    read_write = contract('tn,sn->ts', reader, writer)
    mixing = (decays * read_write[None]).astype(jnp.bfloat16)
    grad_reader = (contract('hts,sn->tn', weighted, writer) + contract('htp,hnp->tn', scaled_cot, state_low)) * norm_scale
    grad_writer = contract('hst,sn->tn', weighted, reader) * norm_scale + contract('htp,hnp->tn', gated_values, adjoint_low)
    carried_part = contract('hst,hsp->htp', mixing, cotangent) * norm_scale
    state_part = to_end[:, :, None] * contract('tn,hnp->htp', writer, adjoint_low)
    grad_values = input_gate[:, :, None] * (carried_part + state_part) + skip_gain[:, None, None] * cotangent.astype(jnp.float32)
    return (grad_values, grad_writer, grad_reader)

def reference(layer_input, proj_weight, state_weight, out_grad, log_decay, skip_gain):
    values_all = jnp.dot(layer_input, proj_weight, preferred_element_type=jnp.float32).astype(jnp.bfloat16)
    projected = jnp.dot(layer_input, state_weight, preferred_element_type=jnp.float32).astype(jnp.bfloat16)
    values = split_heads(values_all, H)
    cotangent = split_heads(out_grad, H)
    block_count = values.shape[0]
    writer = projected[:, :N].reshape(block_count, BLOCK, N)
    reader = projected[:, N:].reshape(block_count, BLOCK, N)
    cumulative, input_gate = decay_blocks(log_decay)
    block_decay, written, pending = lax.map(lambda element: block_summary(*element), (values, cotangent, writer, reader, cumulative, input_gate))
    identity = (jnp.ones((H,), jnp.float32), jnp.zeros((H, N, P_SIZE), jnp.float32))
    final_state, prefix = lax.scan(forward_step, identity, (block_decay, written))
    final_adjoint, suffix = lax.scan(forward_step, identity, (block_decay, pending), reverse=True)
    grad_values, grad_writer, grad_reader = lax.map(lambda element: block_grads(*element, skip_gain), (values, cotangent, writer, reader, cumulative, input_gate, prefix[1], suffix[1]))
    grad_heads = merge_heads(grad_values).astype(jnp.bfloat16)
    grad_projected = jnp.concatenate([grad_writer, grad_reader], axis=2).reshape(block_count * BLOCK, 2 * N).astype(jnp.bfloat16)
    grad_input = (jnp.dot(grad_heads, proj_weight.T, preferred_element_type=jnp.float32) + jnp.dot(grad_projected, state_weight.T, preferred_element_type=jnp.float32)).astype(jnp.bfloat16)
    grad_scale = SEQUENCE_TOKENS ** (-0.5)
    grad_proj = jnp.dot(layer_input.T, grad_heads, preferred_element_type=jnp.float32) * grad_scale
    grad_state = jnp.dot(layer_input.T, grad_projected, preferred_element_type=jnp.float32) * grad_scale
    return (grad_input, grad_proj, grad_state)
```

```python
import functools

import jax
import jax.numpy as jnp
from jax import lax
from jax.experimental import pallas as pl
from jax.experimental.pallas import tpu as pltpu
from jax.sharding import PartitionSpec as P

BLOCK = 256
PAIR = 128
VMEM_LIMIT = 48 * 1024 * 1024


def exchange(array, axis, bit):
    peers = lax.axis_size(axis)
    return lax.ppermute(array, axis, [(i, i ^ bit) for i in range(peers)])


def bits_of(axis):
    peers = lax.axis_size(axis)
    return [1 << k for k in range(peers.bit_length() - 1)]


def has_bit(axis, bit):
    return (lax.axis_index(axis) // bit) % 2


def cube_gather(shard, axis, order):
    bits = bits_of(axis)
    array = shard.reshape((1,) * len(bits) + shard.shape)
    for bit in order:
        dim = len(bits) - bit.bit_length()
        other = exchange(array, axis, bit)
        upper = has_bit(axis, bit) == 1
        array = jnp.concatenate(
            [jnp.where(upper, other, array), jnp.where(upper, array, other)], axis=dim
        )
    return array.reshape((-1,) + shard.shape[1:])


def cube_scatter(partial, axis, order):
    bits = bits_of(axis)
    rows = partial.shape[0] // lax.axis_size(axis)
    array = partial.reshape((2,) * len(bits) + (rows,) + partial.shape[1:])
    for bit in order:
        dim = len(bits) - bit.bit_length()
        own = has_bit(axis, bit)
        keep = lax.dynamic_slice_in_dim(array, own, 1, dim)
        send = lax.dynamic_slice_in_dim(array, 1 - own, 1, dim)
        got = exchange(send, axis, bit)
        total = keep.astype(jnp.float32) + got.astype(jnp.float32)
        array = total.astype(jnp.bfloat16)
    return total.reshape((rows,) + partial.shape[1:])


def per_head(columns, pair):
    low = jnp.broadcast_to(columns[:, 2 * pair : 2 * pair + 1], (columns.shape[0], PAIR // 2))
    high = jnp.broadcast_to(columns[:, 2 * pair + 1 : 2 * pair + 2], (columns.shape[0], PAIR // 2))
    return jnp.concatenate([low, high], axis=1)


def weigh_kernel(x_ref, weight_ref, left_ref, weighted_ref, out_ref):
    weights = weight_ref[0, 0]
    for pair in range(x_ref.shape[1] // PAIR):
        cols = slice(pair * PAIR, (pair + 1) * PAIR)
        scaled = (x_ref[:, cols].astype(jnp.float32) * per_head(weights, pair)).astype(jnp.bfloat16)
        weighted_ref[:, cols] = scaled
        out_ref[0, :, cols] = jnp.dot(left_ref[0], scaled, preferred_element_type=jnp.float32)


def weigh(x, weights, left):
    rows, width = x.shape
    blocks, groups, _, heads = weights.shape
    cols = width // groups
    state = left.shape[1]
    return pl.pallas_call(
        weigh_kernel,
        grid=(blocks, groups),
        in_specs=[
            pl.BlockSpec((BLOCK, cols), lambda b, g: (b, g)),
            pl.BlockSpec((1, 1, BLOCK, heads), lambda b, g: (b, g, 0, 0)),
            pl.BlockSpec((1, state, BLOCK), lambda b, g: (b, 0, 0)),
        ],
        out_specs=[
            pl.BlockSpec((BLOCK, cols), lambda b, g: (b, g)),
            pl.BlockSpec((1, state, cols), lambda b, g: (b, 0, g)),
        ],
        out_shape=[
            jax.ShapeDtypeStruct((rows, width), jnp.bfloat16),
            jax.ShapeDtypeStruct((blocks, state, width), jnp.float32),
        ],
        cost_estimate=pl.CostEstimate(
            flops=2 * rows * width * state, bytes_accessed=6 * rows * width, transcendentals=0
        ),
        compiler_params=pltpu.CompilerParams(vmem_limit_bytes=VMEM_LIMIT),
    )(x, weights, left)


def inner_kernel(
    scale, x_ref, c_ref, cumc_ref, cumr_ref, gate_ref, skip_ref, both_ref,
    part_ref, grads_ref, mix_ref, sum_ref,
):
    group = pl.program_id(1)
    state = both_ref.shape[1] // 2
    writer = both_ref[:, :state]
    reader = both_ref[:, state:]
    cross = (((1,), (1,)), ((), ()))

    @pl.when(group == 0)
    def _():
        mix_ref[...] = lax.dot_general(
            writer, reader, cross, preferred_element_type=jnp.float32
        )
        sum_ref[...] = jnp.zeros_like(sum_ref)

    source = lax.broadcasted_iota(jnp.int32, (BLOCK, BLOCK), 0)
    target = lax.broadcasted_iota(jnp.int32, (BLOCK, BLOCK), 1)
    causal = target >= source
    half = PAIR // 2
    for pair in range(x_ref.shape[1] // PAIR):
        carried = []
        for side in range(2):
            head = 2 * pair + side
            cols = slice(head * half, (head + 1) * half)
            cot = c_ref[:, cols]
            exponent = cumr_ref[0, 0, head : head + 1, :] - cumc_ref[0, 0, :, head : head + 1]
            decays = jnp.exp(jnp.where(causal, exponent, -1e30))
            gram = lax.dot_general(x_ref[:, cols], cot, cross, preferred_element_type=jnp.float32)
            gate = gate_ref[0, 0, :, head : head + 1]
            sum_ref[...] += (decays * gram) * gate
            mixing = (decays * mix_ref[...]).astype(jnp.bfloat16)
            carried.append(
                jnp.dot(mixing, cot, preferred_element_type=jnp.float32) * (gate * scale)
            )
        cols = slice(pair * PAIR, (pair + 1) * PAIR)
        part_ref[:, cols] = jnp.concatenate(carried, axis=1) + skip_ref[:, cols] * c_ref[
            :, cols
        ].astype(jnp.float32)

    @pl.when(group == pl.num_programs(1) - 1)
    def _():
        low = sum_ref[...].astype(jnp.bfloat16)
        grads_ref[:, :state] = scale * jnp.dot(low, reader, preferred_element_type=jnp.float32)
        grads_ref[:, state:] = scale * lax.dot_general(
            low, writer, (((0,), (0,)), ((), ())), preferred_element_type=jnp.float32
        )


def inner(values, cotangent, cum_cols, cum_rows, gate_cols, skip_lanes, projected):
    rows, width = values.shape
    blocks, groups, _, heads = cum_cols.shape
    cols = width // groups
    both = projected.shape[1]
    scale = (both // 2) ** (-0.5)
    column_spec = pl.BlockSpec((1, 1, BLOCK, heads), lambda b, g: (b, g, 0, 0))
    wide = pl.BlockSpec((BLOCK, cols), lambda b, g: (b, g))
    whole = pl.BlockSpec((BLOCK, both), lambda b, g: (b, 0))
    return pl.pallas_call(
        lambda x, c, cc, cr, gt, sk, bo, part, grads, mix, total: inner_kernel(
            scale, x, c, cc, cr, gt, sk, bo, part, grads, mix, total
        ),
        grid=(blocks, groups),
        in_specs=[
            wide,
            wide,
            column_spec,
            pl.BlockSpec((1, 1, heads, BLOCK), lambda b, g: (b, g, 0, 0)),
            column_spec,
            pl.BlockSpec((1, cols), lambda b, g: (0, g)),
            whole,
        ],
        out_specs=[wide, whole],
        out_shape=[
            jax.ShapeDtypeStruct((rows, width), jnp.float32),
            jax.ShapeDtypeStruct((rows, both), jnp.float32),
        ],
        scratch_shapes=[
            pltpu.VMEM((BLOCK, BLOCK), jnp.float32),
            pltpu.VMEM((BLOCK, BLOCK), jnp.float32),
        ],
        cost_estimate=pl.CostEstimate(
            flops=16 * rows * width * BLOCK, bytes_accessed=8 * rows * width, transcendentals=0
        ),
        compiler_params=pltpu.CompilerParams(vmem_limit_bytes=VMEM_LIMIT),
    )(values, cotangent, cum_cols, cum_rows, gate_cols, skip_lanes, projected)


def outer_kernel(
    scale, gated_ref, scaled_ref, part_ref, weight_ref, both_ref, inner_ref, state_ref, adjoint_ref,
    heads_ref, grads_ref,
):
    group = pl.program_id(1)
    state = both_ref.shape[1] // 2
    writer = both_ref[:, :state]
    adjoint = adjoint_ref[0]
    cross = (((1,), (1,)), ((), ()))

    @pl.when(group == 0)
    def _():
        grads_ref[...] = inner_ref[...]

    grads_ref[:, :state] += lax.dot_general(
        gated_ref[...], adjoint, cross, preferred_element_type=jnp.float32
    )
    grads_ref[:, state:] += scale * lax.dot_general(
        scaled_ref[...], state_ref[0], cross, preferred_element_type=jnp.float32
    )
    weights = weight_ref[0, 0]
    for pair in range(gated_ref.shape[1] // PAIR):
        cols = slice(pair * PAIR, (pair + 1) * PAIR)
        entering = jnp.dot(writer, adjoint[:, cols], preferred_element_type=jnp.float32)
        total = part_ref[:, cols] + per_head(weights, pair) * entering
        heads_ref[:, cols] = total.astype(jnp.bfloat16)


def outer(gated, scaled, part, weight_cols, projected, inner_grads, state_in, adjoint_in):
    rows, width = gated.shape
    blocks, groups, _, heads = weight_cols.shape
    cols = width // groups
    both = projected.shape[1]
    state = both // 2
    wide = pl.BlockSpec((BLOCK, cols), lambda b, g: (b, g))
    whole = pl.BlockSpec((BLOCK, both), lambda b, g: (b, 0))
    carried = pl.BlockSpec((1, state, cols), lambda b, g: (b, 0, g))
    return pl.pallas_call(
        functools.partial(outer_kernel, state ** (-0.5)),
        grid=(blocks, groups),
        in_specs=[
            wide,
            wide,
            wide,
            pl.BlockSpec((1, 1, BLOCK, heads), lambda b, g: (b, g, 0, 0)),
            whole,
            whole,
            carried,
            carried,
        ],
        out_specs=[wide, whole],
        out_shape=[
            jax.ShapeDtypeStruct((rows, width), jnp.bfloat16),
            jax.ShapeDtypeStruct((rows, both), jnp.float32),
        ],
        cost_estimate=pl.CostEstimate(
            flops=6 * rows * width * state, bytes_accessed=10 * rows * width, transcendentals=0
        ),
        compiler_params=pltpu.CompilerParams(vmem_limit_bytes=VMEM_LIMIT),
    )(gated, scaled, part, weight_cols, projected, inner_grads, state_in, adjoint_in)


def arriving(total, logs, lanes, forward):
    peers = lax.axis_size("ctx")
    me = lax.axis_index("ctx")
    index = jnp.arange(peers)

    def decay(first, last):
        inside = ((index >= first) & (index < last))[:, None]
        return jnp.exp(lanes(jnp.sum(jnp.where(inside, logs, 0.0), axis=0)))[None, :]

    entering = jnp.zeros_like(total)
    for bit in bits_of("ctx"):
        got = exchange(total.astype(jnp.bfloat16), "ctx", bit).astype(jnp.float32)
        start = (me // bit) * bit
        upper = has_bit("ctx", bit) == 1
        takes = upper if forward else jnp.logical_not(upper)
        between = decay(start, me) if forward else decay(me + 1, start + bit)
        entering = entering + jnp.where(takes, between * got, 0.0)
        partner = start ^ bit
        far_first = jnp.where(takes, start, partner)
        passed = decay(far_first, far_first + bit)
        total = jnp.where(takes, got, total) * passed + jnp.where(takes, total, got)
    return entering


def entering_blocks(terms, block_decay, arrived, forward):
    blocks = terms.shape[0]
    order = range(blocks) if forward else range(blocks - 1, -1, -1)
    held = [None] * blocks
    carried = arrived
    for block in order:
        held[block] = carried.astype(jnp.bfloat16)
        carried = block_decay[block][None, :] * carried + terms[block]
    return jnp.stack(held)


def piece_total(terms, block_decay, forward):
    blocks = terms.shape[0]
    order = range(blocks) if forward else range(blocks - 1, -1, -1)
    total = None
    for block in order:
        total = terms[block] if total is None else block_decay[block][None, :] * total + terms[block]
    return total


def shards(layer_input, proj_weight, state_weight, out_grad, log_decay, skip_gain):
    heads = skip_gain.shape[0]
    width = out_grad.shape[1]
    head_width = width // heads
    blocks = out_grad.shape[0] // BLOCK
    state = state_weight.shape[1] // 2
    scale = state ** (-0.5)
    groups = max(1, heads // 10)
    bits = bits_of("ctx")
    high = bits[1:]

    def lanes(per_head_values):
        return jnp.repeat(per_head_values, head_width, axis=-1)

    gathered = lax.all_gather(layer_input, "sp", axis=0, tiled=True)
    half = width // 2
    weight_a = cube_gather(proj_weight[:, :half], "ctx", high + bits[:1])
    weight_b = cube_gather(proj_weight[:, half:], "ctx", high[::-1] + bits[:1])

    shaped = log_decay.reshape(groups, heads // groups, blocks, BLOCK)
    cum_rows = jnp.cumsum(shaped, axis=3).transpose(2, 0, 1, 3)
    gate_rows = jnp.sqrt(-jnp.expm1(2.0 * shaped)).transpose(2, 0, 1, 3)
    to_end_rows = jnp.exp(cum_rows[..., -1:] - cum_rows)
    block_logs = cum_rows[..., -1].reshape(blocks, heads)
    block_decay = jnp.exp(lanes(block_logs))
    logs = cube_gather(jnp.sum(block_logs, axis=0)[None], "ctx", bits)
    cum_cols = cum_rows.transpose(0, 1, 3, 2)
    gate_cols = gate_rows.transpose(0, 1, 3, 2)
    from_start_cols = jnp.exp(cum_cols)
    gate_end_cols = (gate_rows * to_end_rows).transpose(0, 1, 3, 2)

    projected = jnp.dot(gathered, state_weight, preferred_element_type=jnp.float32).astype(
        jnp.bfloat16
    )
    turned = projected.reshape(blocks, BLOCK, 2 * state).transpose(0, 2, 1)
    scaled_cot, pending = weigh(out_grad, from_start_cols, turned[:, state:])
    pending = pending * scale
    adjoint_from = arriving(piece_total(pending, block_decay, False), logs, lanes, False)

    values = jnp.concatenate(
        [
            jnp.dot(gathered, w, preferred_element_type=jnp.float32).astype(jnp.bfloat16)
            for w in (weight_a, weight_b)
        ],
        axis=1,
    )
    gated, written = weigh(values, gate_end_cols, turned[:, :state])
    state_from = arriving(piece_total(written, block_decay, True), logs, lanes, True)
    part, inner_grads = inner(
        values, out_grad, cum_cols, cum_rows, gate_cols, lanes(skip_gain)[None, :], projected
    )
    state_in = entering_blocks(written, block_decay, state_from, True)
    adjoint_in = entering_blocks(pending, block_decay, adjoint_from, False)
    grad_heads, partial_grads = outer(
        gated, scaled_cot, part, gate_end_cols, projected, inner_grads, state_in, adjoint_in
    )
    low_grads = partial_grads.astype(jnp.bfloat16)

    across = (((1,), (1,)), ((), ()))
    down = (((0,), (0,)), ((), ()))
    dot = functools.partial(lax.dot_general, preferred_element_type=jnp.float32)
    grad_input = lax.psum_scatter(
        (
            dot(grad_heads[:, :half], weight_a, across)
            + dot(grad_heads[:, half:], weight_b, across)
            + dot(low_grads, state_weight, across)
        ).astype(jnp.bfloat16),
        "sp",
        scatter_dimension=0,
        tiled=True,
    )
    grad_scale = (gathered.shape[0] * lax.axis_size("ctx")) ** (-0.5)
    term_a = dot(gathered, grad_heads[:, :half], down).astype(jnp.bfloat16)
    term_b = dot(gathered, grad_heads[:, half:], down).astype(jnp.bfloat16)
    term_s = dot(gathered, low_grads, down).astype(jnp.bfloat16)
    sum_a = cube_scatter(term_a, "ctx", bits[:1] + high)
    sum_b = cube_scatter(term_b, "ctx", bits[:1] + high[::-1])
    sum_s = cube_scatter(term_s, "ctx", bits)
    grad_proj = jnp.concatenate([sum_a, sum_b], axis=1) * grad_scale
    grad_state = cube_scatter(sum_s.astype(jnp.bfloat16), "sp", bits_of("sp")) * grad_scale
    return (grad_input, grad_proj, grad_state)


def solution(mesh):
    in_specs = (
        P(("ctx", "sp"), None),
        P("ctx", "sp"),
        P(),
        P("ctx", "sp"),
        P("sp", "ctx"),
        P("sp"),
    )
    out_specs = (P(("ctx", "sp"), None), P("ctx", "sp"), P(("ctx", "sp"), None))
    return jax.shard_map(shards, mesh=mesh, in_specs=in_specs, out_specs=out_specs, check_vma=False)
```

```python
import functools

import jax
import jax.numpy as jnp
from jax import lax
from jax.experimental import pallas as pl
from jax.experimental.pallas import tpu as pltpu
from jax.sharding import PartitionSpec as P

BLOCK = 256
PAIR = 128
VMEM_LIMIT = 48 * 1024 * 1024


def exchange(array, axis, bit):
    peers = lax.axis_size(axis)
    return lax.ppermute(array, axis, [(i, i ^ bit) for i in range(peers)])


def bits_of(axis):
    peers = lax.axis_size(axis)
    return [1 << k for k in range(peers.bit_length() - 1)]


def has_bit(axis, bit):
    return (lax.axis_index(axis) // bit) % 2


def cube_gather(shard, axis, order):
    bits = bits_of(axis)
    array = shard.reshape((1,) * len(bits) + shard.shape)
    for bit in order:
        dim = len(bits) - bit.bit_length()
        other = exchange(array, axis, bit)
        upper = has_bit(axis, bit) == 1
        array = jnp.concatenate(
            [jnp.where(upper, other, array), jnp.where(upper, array, other)], axis=dim
        )
    return array.reshape((-1,) + shard.shape[1:])


def cube_scatter(partial, axis, order):
    bits = bits_of(axis)
    rows = partial.shape[0] // lax.axis_size(axis)
    array = partial.reshape((2,) * len(bits) + (rows,) + partial.shape[1:])
    for bit in order:
        dim = len(bits) - bit.bit_length()
        own = has_bit(axis, bit)
        keep = lax.dynamic_slice_in_dim(array, own, 1, dim)
        send = lax.dynamic_slice_in_dim(array, 1 - own, 1, dim)
        got = exchange(send, axis, bit)
        total = keep.astype(jnp.float32) + got.astype(jnp.float32)
        array = total.astype(jnp.bfloat16)
    return total.reshape((rows,) + partial.shape[1:])


def per_head(columns, pair):
    low = jnp.broadcast_to(columns[:, 2 * pair : 2 * pair + 1], (columns.shape[0], PAIR // 2))
    high = jnp.broadcast_to(columns[:, 2 * pair + 1 : 2 * pair + 2], (columns.shape[0], PAIR // 2))
    return jnp.concatenate([low, high], axis=1)


def weigh_kernel(x_ref, weight_ref, left_ref, weighted_ref, out_ref):
    weights = weight_ref[0, 0]
    for pair in range(x_ref.shape[1] // PAIR):
        cols = slice(pair * PAIR, (pair + 1) * PAIR)
        scaled = (x_ref[:, cols].astype(jnp.float32) * per_head(weights, pair)).astype(jnp.bfloat16)
        weighted_ref[:, cols] = scaled
        out_ref[0, :, cols] = jnp.dot(left_ref[0], scaled, preferred_element_type=jnp.float32)


def weigh(x, weights, left):
    rows, width = x.shape
    blocks, groups, _, heads = weights.shape
    cols = width // groups
    state = left.shape[1]
    return pl.pallas_call(
        weigh_kernel,
        grid=(blocks, groups),
        in_specs=[
            pl.BlockSpec((BLOCK, cols), lambda b, g: (b, g)),
            pl.BlockSpec((1, 1, BLOCK, heads), lambda b, g: (b, g, 0, 0)),
            pl.BlockSpec((1, state, BLOCK), lambda b, g: (b, 0, 0)),
        ],
        out_specs=[
            pl.BlockSpec((BLOCK, cols), lambda b, g: (b, g)),
            pl.BlockSpec((1, state, cols), lambda b, g: (b, 0, g)),
        ],
        out_shape=[
            jax.ShapeDtypeStruct((rows, width), jnp.bfloat16),
            jax.ShapeDtypeStruct((blocks, state, width), jnp.float32),
        ],
        cost_estimate=pl.CostEstimate(
            flops=2 * rows * width * state, bytes_accessed=6 * rows * width, transcendentals=0
        ),
        compiler_params=pltpu.CompilerParams(vmem_limit_bytes=VMEM_LIMIT),
    )(x, weights, left)


def inner_kernel(
    scale, x_ref, c_ref, cumc_ref, cumr_ref, gate_ref, skip_ref, both_ref,
    part_ref, grads_ref, mix_ref, sum_ref,
):
    group = pl.program_id(1)
    state = both_ref.shape[1] // 2
    writer = both_ref[:, :state]
    reader = both_ref[:, state:]
    cross = (((1,), (1,)), ((), ()))

    @pl.when(group == 0)
    def _():
        mix_ref[...] = lax.dot_general(
            writer, reader, cross, preferred_element_type=jnp.float32
        )
        sum_ref[...] = jnp.zeros_like(sum_ref)

    source = lax.broadcasted_iota(jnp.int32, (BLOCK, BLOCK), 0)
    target = lax.broadcasted_iota(jnp.int32, (BLOCK, BLOCK), 1)
    causal = target >= source
    half = PAIR // 2
    for pair in range(x_ref.shape[1] // PAIR):
        carried = []
        for side in range(2):
            head = 2 * pair + side
            cols = slice(head * half, (head + 1) * half)
            cot = c_ref[:, cols]
            exponent = cumr_ref[0, 0, head : head + 1, :] - cumc_ref[0, 0, :, head : head + 1]
            decays = jnp.exp(jnp.where(causal, exponent, -1e30))
            gram = lax.dot_general(x_ref[:, cols], cot, cross, preferred_element_type=jnp.float32)
            gate = gate_ref[0, 0, :, head : head + 1]
            sum_ref[...] += (decays * gram) * gate
            mixing = (decays * mix_ref[...]).astype(jnp.bfloat16)
            carried.append(
                jnp.dot(mixing, cot, preferred_element_type=jnp.float32) * (gate * scale)
            )
        cols = slice(pair * PAIR, (pair + 1) * PAIR)
        part_ref[:, cols] = jnp.concatenate(carried, axis=1) + skip_ref[:, cols] * c_ref[
            :, cols
        ].astype(jnp.float32)

    @pl.when(group == pl.num_programs(1) - 1)
    def _():
        low = sum_ref[...].astype(jnp.bfloat16)
        grads_ref[:, :state] = scale * jnp.dot(low, reader, preferred_element_type=jnp.float32)
        grads_ref[:, state:] = scale * lax.dot_general(
            low, writer, (((0,), (0,)), ((), ())), preferred_element_type=jnp.float32
        )


def inner(values, cotangent, cum_cols, cum_rows, gate_cols, skip_lanes, projected):
    rows, width = values.shape
    blocks, groups, _, heads = cum_cols.shape
    cols = width // groups
    both = projected.shape[1]
    scale = (both // 2) ** (-0.5)
    column_spec = pl.BlockSpec((1, 1, BLOCK, heads), lambda b, g: (b, g, 0, 0))
    wide = pl.BlockSpec((BLOCK, cols), lambda b, g: (b, g))
    whole = pl.BlockSpec((BLOCK, both), lambda b, g: (b, 0))
    return pl.pallas_call(
        lambda x, c, cc, cr, gt, sk, bo, part, grads, mix, total: inner_kernel(
            scale, x, c, cc, cr, gt, sk, bo, part, grads, mix, total
        ),
        grid=(blocks, groups),
        in_specs=[
            wide,
            wide,
            column_spec,
            pl.BlockSpec((1, 1, heads, BLOCK), lambda b, g: (b, g, 0, 0)),
            column_spec,
            pl.BlockSpec((1, cols), lambda b, g: (0, g)),
            whole,
        ],
        out_specs=[wide, whole],
        out_shape=[
            jax.ShapeDtypeStruct((rows, width), jnp.float32),
            jax.ShapeDtypeStruct((rows, both), jnp.float32),
        ],
        scratch_shapes=[
            pltpu.VMEM((BLOCK, BLOCK), jnp.float32),
            pltpu.VMEM((BLOCK, BLOCK), jnp.float32),
        ],
        cost_estimate=pl.CostEstimate(
            flops=16 * rows * width * BLOCK, bytes_accessed=8 * rows * width, transcendentals=0
        ),
        compiler_params=pltpu.CompilerParams(vmem_limit_bytes=VMEM_LIMIT),
    )(values, cotangent, cum_cols, cum_rows, gate_cols, skip_lanes, projected)


def outer_kernel(
    scale, gated_ref, scaled_ref, part_ref, weight_ref, both_ref, inner_ref, state_ref, adjoint_ref,
    heads_ref, grads_ref,
):
    group = pl.program_id(1)
    state = both_ref.shape[1] // 2
    writer = both_ref[:, :state]
    adjoint = adjoint_ref[0]
    cross = (((1,), (1,)), ((), ()))

    @pl.when(group == 0)
    def _():
        grads_ref[...] = inner_ref[...]

    grads_ref[:, :state] += lax.dot_general(
        gated_ref[...], adjoint, cross, preferred_element_type=jnp.float32
    )
    grads_ref[:, state:] += scale * lax.dot_general(
        scaled_ref[...], state_ref[0], cross, preferred_element_type=jnp.float32
    )
    weights = weight_ref[0, 0]
    for pair in range(gated_ref.shape[1] // PAIR):
        cols = slice(pair * PAIR, (pair + 1) * PAIR)
        entering = jnp.dot(writer, adjoint[:, cols], preferred_element_type=jnp.float32)
        total = part_ref[:, cols] + per_head(weights, pair) * entering
        heads_ref[:, cols] = total.astype(jnp.bfloat16)


def outer(gated, scaled, part, weight_cols, projected, inner_grads, state_in, adjoint_in):
    rows, width = gated.shape
    blocks, groups, _, heads = weight_cols.shape
    cols = width // groups
    both = projected.shape[1]
    state = both // 2
    wide = pl.BlockSpec((BLOCK, cols), lambda b, g: (b, g))
    whole = pl.BlockSpec((BLOCK, both), lambda b, g: (b, 0))
    carried = pl.BlockSpec((1, state, cols), lambda b, g: (b, 0, g))
    return pl.pallas_call(
        functools.partial(outer_kernel, state ** (-0.5)),
        grid=(blocks, groups),
        in_specs=[
            wide,
            wide,
            wide,
            pl.BlockSpec((1, 1, BLOCK, heads), lambda b, g: (b, g, 0, 0)),
            whole,
            whole,
            carried,
            carried,
        ],
        out_specs=[wide, whole],
        out_shape=[
            jax.ShapeDtypeStruct((rows, width), jnp.bfloat16),
            jax.ShapeDtypeStruct((rows, both), jnp.float32),
        ],
        cost_estimate=pl.CostEstimate(
            flops=6 * rows * width * state, bytes_accessed=10 * rows * width, transcendentals=0
        ),
        compiler_params=pltpu.CompilerParams(vmem_limit_bytes=VMEM_LIMIT),
    )(gated, scaled, part, weight_cols, projected, inner_grads, state_in, adjoint_in)


def span_logs(logs, first, last):
    index = jnp.arange(logs.shape[0])
    inside = ((index >= first) & (index < last))[:, None]
    return jnp.sum(jnp.where(inside, logs, 0.0), axis=0)


def step_logs(logs, forward):
    me = lax.axis_index("ctx")
    rows = []
    for bit in bits_of("ctx"):
        start = (me // bit) * bit
        takes = has_bit("ctx", bit) == (1 if forward else 0)
        far_first = jnp.where(takes, start, start ^ bit)
        rows.append(span_logs(logs, start, me) if forward else span_logs(logs, me + 1, start + bit))
        rows.append(span_logs(logs, far_first, far_first + bit))
    return rows


def arriving_step(carried, bit, between, passed, forward):
    total, entering = carried
    got = exchange(total.astype(jnp.bfloat16), "ctx", bit).astype(jnp.float32)
    takes = has_bit("ctx", bit) == (1 if forward else 0)
    entering = entering + jnp.where(takes, between[None] * got, 0.0)
    total = jnp.where(takes, got, total) * passed[None] + jnp.where(takes, total, got)
    return (total, entering)


def chain_gather(shard, axis):
    peers = lax.axis_size(axis)
    me = lax.axis_index(axis)
    rows = shard.shape[0]
    full = jnp.zeros((peers * rows,) + shard.shape[1:], shard.dtype)
    from_left = from_right = shard
    arrived = []
    for step in range(1, peers):
        from_left = lax.ppermute(from_left, axis, [(i, i + 1) for i in range(peers - 1)])
        from_right = lax.ppermute(from_right, axis, [(i, i - 1) for i in range(1, peers)])
        arrived += [(from_left, me - step), (from_right, me + step)]
    for piece, owner in arrived:
        place = jnp.where((owner >= 0) & (owner < peers), owner, me)
        full = lax.dynamic_update_slice_in_dim(full, piece, place * rows, 0)
    return lax.dynamic_update_slice_in_dim(full, shard, me * rows, 0)


def entering_blocks(terms, block_decay, arrived, forward):
    blocks = terms.shape[0]
    order = range(blocks) if forward else range(blocks - 1, -1, -1)
    held = [None] * blocks
    carried = arrived
    for block in order:
        held[block] = carried.astype(jnp.bfloat16)
        carried = block_decay[block][None, :] * carried + terms[block]
    return jnp.stack(held)


def piece_total(terms, block_decay, forward):
    blocks = terms.shape[0]
    order = range(blocks) if forward else range(blocks - 1, -1, -1)
    total = None
    for block in order:
        total = terms[block] if total is None else block_decay[block][None, :] * total + terms[block]
    return total


def product_kernel(left_ref, right_ref, out_ref):
    out_ref[...] = jnp.dot(
        left_ref[...], right_ref[...], preferred_element_type=jnp.float32
    ).astype(jnp.bfloat16)


def columns_product(left, right, first, width):
    rows, depth = left.shape
    tile = rows // 5
    if width % PAIR:
        right, first = right[:, first : first + width], 0
    return pl.pallas_call(
        product_kernel,
        grid=(rows // tile,),
        in_specs=[
            pl.BlockSpec((tile, depth), lambda i: (i, 0)),
            pl.BlockSpec((depth, width), lambda i: (0, first // width)),
        ],
        out_specs=pl.BlockSpec((tile, width), lambda i: (i, 0)),
        out_shape=jax.ShapeDtypeStruct((rows, width), jnp.bfloat16),
        cost_estimate=pl.CostEstimate(
            flops=2 * rows * depth * width,
            bytes_accessed=2 * (rows * depth + rows * width + depth * width),
            transcendentals=0,
        ),
        compiler_params=pltpu.CompilerParams(vmem_limit_bytes=VMEM_LIMIT),
    )(left, right)


def shards(layer_input, proj_weight, state_weight, out_grad, log_decay, skip_gain):
    heads = skip_gain.shape[0]
    width = out_grad.shape[1]
    head_width = width // heads
    blocks = out_grad.shape[0] // BLOCK
    state = state_weight.shape[1] // 2
    scale = state ** (-0.5)
    groups = max(1, heads // 10)
    bits = bits_of("ctx")
    high = bits[1:]

    def lanes(per_head_values):
        return jnp.repeat(per_head_values, head_width, axis=-1)

    full_weight = lax.all_gather(proj_weight, "ctx", axis=0, tiled=True)
    gathered = chain_gather(layer_input, "sp")
    half = width // 2

    shaped = log_decay.reshape(groups, heads // groups, blocks, BLOCK)
    cum_rows = jnp.cumsum(shaped, axis=3).transpose(2, 0, 1, 3)
    gate_rows = jnp.sqrt(-jnp.expm1(2.0 * shaped)).transpose(2, 0, 1, 3)
    to_end_rows = jnp.exp(cum_rows[..., -1:] - cum_rows)
    block_logs = cum_rows[..., -1].reshape(blocks, heads)
    logs = cube_gather(jnp.sum(block_logs, axis=0)[None], "ctx", bits)
    ahead, back = step_logs(logs, True), step_logs(logs, False)
    factors = lanes(jnp.exp(jnp.stack(list(block_logs) + ahead + back)))
    cum_cols = cum_rows.transpose(0, 1, 3, 2)
    gate_cols = gate_rows.transpose(0, 1, 3, 2)
    from_start_cols = jnp.exp(cum_cols)
    gate_end_cols = (gate_rows * to_end_rows).transpose(0, 1, 3, 2)

    skip_lanes = lanes(skip_gain)[None, :]
    factors, skip_lanes, cum_cols, cum_rows, gate_cols, from_start_cols, gate_end_cols, gathered = (
        lax.optimization_barrier(
            (
                factors,
                skip_lanes,
                cum_cols,
                cum_rows,
                gate_cols,
                from_start_cols,
                gate_end_cols,
                gathered,
            )
        )
    )
    block_decay = factors[:blocks]
    ahead = factors[blocks : blocks + len(ahead)]
    back = factors[blocks + len(ahead) :]

    def step(carried, number, forward):
        rows = ahead if forward else back
        return arriving_step(
            carried, bits[number], rows[2 * number], rows[2 * number + 1], forward
        )

    projected = jnp.dot(gathered, state_weight, preferred_element_type=jnp.float32).astype(
        jnp.bfloat16
    )
    turned = projected.reshape(blocks, BLOCK, 2 * state).transpose(0, 2, 1)
    scaled_cot, pending = weigh(out_grad, from_start_cols, turned[:, state:])
    pending = pending * scale
    total = piece_total(pending, block_decay, False)
    adjoint = step((total, jnp.zeros_like(total)), 0, False)
    adjoint, gathered = lax.optimization_barrier((adjoint, gathered))
    values = jnp.dot(gathered, full_weight, preferred_element_type=jnp.float32).astype(jnp.bfloat16)
    adjoint = step(adjoint, 1, False)
    gated, written = weigh(values, gate_end_cols, turned[:, :state])
    total = piece_total(written, block_decay, True)
    arriving = step((total, jnp.zeros_like(total)), 0, True)
    adjoint, arriving, values = lax.optimization_barrier((adjoint, arriving, values))
    for number in range(2, len(bits)):
        adjoint = step(adjoint, number, False)
    for number in range(1, len(bits)):
        arriving = step(arriving, number, True)
    state_from, adjoint_from = arriving[1], adjoint[1]
    part, inner_grads = inner(
        values, out_grad, cum_cols, cum_rows, gate_cols, skip_lanes, projected
    )
    state_in = entering_blocks(written, block_decay, state_from, True)
    adjoint_in = entering_blocks(pending, block_decay, adjoint_from, False)
    grad_heads, partial_grads = outer(
        gated, scaled_cot, part, gate_end_cols, projected, inner_grads, state_in, adjoint_in
    )
    low_grads = partial_grads.astype(jnp.bfloat16)

    turned_input = lax.optimization_barrier(gathered.T)
    across = (((1,), (1,)), ((), ()))
    dot = functools.partial(lax.dot_general, preferred_element_type=jnp.float32)
    input_terms = (
        dot(grad_heads, full_weight, across) + dot(low_grads, state_weight, across)
    ).astype(jnp.bfloat16)
    input_terms, turned_input = lax.optimization_barrier((input_terms, turned_input))
    grad_input = lax.psum_scatter(input_terms, "sp", scatter_dimension=0, tiled=True)
    grad_scale = (gathered.shape[0] * lax.axis_size("ctx")) ** (-0.5)
    term_a = columns_product(turned_input, grad_heads, 0, half)
    term_b = columns_product(turned_input, grad_heads, half, half)
    term_s = columns_product(turned_input, low_grads, 0, 2 * state)
    sum_a = cube_scatter(term_a, "ctx", bits[:1] + high)
    sum_b = cube_scatter(term_b, "ctx", bits[:1] + high[::-1])
    sum_s = cube_scatter(term_s, "ctx", bits)
    grad_proj = jnp.concatenate([sum_a, sum_b], axis=1) * grad_scale
    grad_state = cube_scatter(sum_s.astype(jnp.bfloat16), "sp", bits_of("sp")) * grad_scale
    return (grad_input, grad_proj, grad_state)


def solution(mesh):
    in_specs = (
        P(("ctx", "sp"), None),
        P("ctx", "sp"),
        P(),
        P("ctx", "sp"),
        P("sp", "ctx"),
        P("sp"),
    )
    out_specs = (P(("ctx", "sp"), None), P("ctx", "sp"), P(("ctx", "sp"), None))
    return jax.shard_map(shards, mesh=mesh, in_specs=in_specs, out_specs=out_specs, check_vma=False)
```

```python
import functools

import jax
import jax.numpy as jnp
from jax import lax
from jax.experimental import pallas as pl
from jax.experimental.pallas import tpu as pltpu
from jax.sharding import PartitionSpec as P

BLOCK = 256
PAIR = 128
VMEM_LIMIT = 48 * 1024 * 1024


def exchange(array, axis, bit):
    peers = lax.axis_size(axis)
    return lax.ppermute(array, axis, [(i, i ^ bit) for i in range(peers)])


def bits_of(axis):
    peers = lax.axis_size(axis)
    return [1 << k for k in range(peers.bit_length() - 1)]


def has_bit(axis, bit):
    return (lax.axis_index(axis) // bit) % 2


def cube_gather(shard, axis, order):
    bits = bits_of(axis)
    array = shard.reshape((1,) * len(bits) + shard.shape)
    for bit in order:
        dim = len(bits) - bit.bit_length()
        other = exchange(array, axis, bit)
        upper = has_bit(axis, bit) == 1
        array = jnp.concatenate(
            [jnp.where(upper, other, array), jnp.where(upper, array, other)], axis=dim
        )
    return array.reshape((-1,) + shard.shape[1:])


def cube_scatter(keep, send, axis, order):
    bits = bits_of(axis)
    rows = 2 * keep.shape[0] // lax.axis_size(axis)
    total = keep.astype(jnp.float32) + exchange(send, axis, 1).astype(jnp.float32)
    total = total.reshape((2,) * (len(bits) - 1) + (rows,) + keep.shape[1:])
    for bit in order:
        dim = len(bits) - bit.bit_length()
        own = has_bit(axis, bit)
        array = total.astype(jnp.bfloat16)
        keep = lax.dynamic_slice_in_dim(array, own, 1, dim)
        send = lax.dynamic_slice_in_dim(array, 1 - own, 1, dim)
        got = exchange(send, axis, bit)
        total = keep.astype(jnp.float32) + got.astype(jnp.float32)
    return total.reshape((rows,) + total.shape[len(bits) :])


def per_head(columns, pair):
    low = jnp.broadcast_to(columns[:, 2 * pair : 2 * pair + 1], (columns.shape[0], PAIR // 2))
    high = jnp.broadcast_to(columns[:, 2 * pair + 1 : 2 * pair + 2], (columns.shape[0], PAIR // 2))
    return jnp.concatenate([low, high], axis=1)


def weigh_kernel(x_ref, weight_ref, left_ref, weighted_ref, out_ref):
    weights = weight_ref[0, 0]
    for pair in range(x_ref.shape[1] // PAIR):
        cols = slice(pair * PAIR, (pair + 1) * PAIR)
        scaled = (x_ref[:, cols].astype(jnp.float32) * per_head(weights, pair)).astype(jnp.bfloat16)
        weighted_ref[:, cols] = scaled
        out_ref[0, :, cols] = jnp.dot(left_ref[0], scaled, preferred_element_type=jnp.float32)


def weigh(x, weights, left):
    rows, width = x.shape
    blocks, groups, _, heads = weights.shape
    cols = width // groups
    state = left.shape[1]
    return pl.pallas_call(
        weigh_kernel,
        grid=(blocks, groups),
        in_specs=[
            pl.BlockSpec((BLOCK, cols), lambda b, g: (b, g)),
            pl.BlockSpec((1, 1, BLOCK, heads), lambda b, g: (b, g, 0, 0)),
            pl.BlockSpec((1, state, BLOCK), lambda b, g: (b, 0, 0)),
        ],
        out_specs=[
            pl.BlockSpec((BLOCK, cols), lambda b, g: (b, g)),
            pl.BlockSpec((1, state, cols), lambda b, g: (b, 0, g)),
        ],
        out_shape=[
            jax.ShapeDtypeStruct((rows, width), jnp.bfloat16),
            jax.ShapeDtypeStruct((blocks, state, width), jnp.float32),
        ],
        cost_estimate=pl.CostEstimate(
            flops=2 * rows * width * state, bytes_accessed=6 * rows * width, transcendentals=0
        ),
        compiler_params=pltpu.CompilerParams(vmem_limit_bytes=VMEM_LIMIT),
    )(x, weights, left)


def inner_kernel(
    scale, x_ref, c_ref, cumc_ref, cumr_ref, gate_ref, skip_ref, both_ref,
    part_ref, grads_ref, mix_ref, sum_ref,
):
    group = pl.program_id(1)
    state = both_ref.shape[1] // 2
    writer = both_ref[:, :state]
    reader = both_ref[:, state:]
    cross = (((1,), (1,)), ((), ()))

    @pl.when(group == 0)
    def _():
        mix_ref[...] = lax.dot_general(
            writer, reader, cross, preferred_element_type=jnp.float32
        )
        sum_ref[...] = jnp.zeros_like(sum_ref)

    source = lax.broadcasted_iota(jnp.int32, (BLOCK, BLOCK), 0)
    target = lax.broadcasted_iota(jnp.int32, (BLOCK, BLOCK), 1)
    causal = target >= source
    half = PAIR // 2
    for pair in range(x_ref.shape[1] // PAIR):
        carried = []
        for side in range(2):
            head = 2 * pair + side
            cols = slice(head * half, (head + 1) * half)
            cot = c_ref[:, cols]
            exponent = cumr_ref[0, 0, head : head + 1, :] - cumc_ref[0, 0, :, head : head + 1]
            decays = jnp.exp(jnp.where(causal, exponent, -1e30))
            gram = lax.dot_general(x_ref[:, cols], cot, cross, preferred_element_type=jnp.float32)
            gate = gate_ref[0, 0, :, head : head + 1]
            sum_ref[...] += (decays * gram) * gate
            mixing = (decays * mix_ref[...]).astype(jnp.bfloat16)
            carried.append(
                jnp.dot(mixing, cot, preferred_element_type=jnp.float32) * (gate * scale)
            )
        cols = slice(pair * PAIR, (pair + 1) * PAIR)
        part_ref[:, cols] = jnp.concatenate(carried, axis=1) + skip_ref[:, cols] * c_ref[
            :, cols
        ].astype(jnp.float32)

    @pl.when(group == pl.num_programs(1) - 1)
    def _():
        low = sum_ref[...].astype(jnp.bfloat16)
        grads_ref[:, :state] = scale * jnp.dot(low, reader, preferred_element_type=jnp.float32)
        grads_ref[:, state:] = scale * lax.dot_general(
            low, writer, (((0,), (0,)), ((), ())), preferred_element_type=jnp.float32
        )


def inner(values, cotangent, cum_cols, cum_rows, gate_cols, skip_lanes, projected):
    rows, width = values.shape
    blocks, groups, _, heads = cum_cols.shape
    cols = width // groups
    both = projected.shape[1]
    scale = (both // 2) ** (-0.5)
    column_spec = pl.BlockSpec((1, 1, BLOCK, heads), lambda b, g: (b, g, 0, 0))
    wide = pl.BlockSpec((BLOCK, cols), lambda b, g: (b, g))
    whole = pl.BlockSpec((BLOCK, both), lambda b, g: (b, 0))
    return pl.pallas_call(
        lambda x, c, cc, cr, gt, sk, bo, part, grads, mix, total: inner_kernel(
            scale, x, c, cc, cr, gt, sk, bo, part, grads, mix, total
        ),
        grid=(blocks, groups),
        in_specs=[
            wide,
            wide,
            column_spec,
            pl.BlockSpec((1, 1, heads, BLOCK), lambda b, g: (b, g, 0, 0)),
            column_spec,
            pl.BlockSpec((1, cols), lambda b, g: (0, g)),
            whole,
        ],
        out_specs=[wide, whole],
        out_shape=[
            jax.ShapeDtypeStruct((rows, width), jnp.float32),
            jax.ShapeDtypeStruct((rows, both), jnp.float32),
        ],
        scratch_shapes=[
            pltpu.VMEM((BLOCK, BLOCK), jnp.float32),
            pltpu.VMEM((BLOCK, BLOCK), jnp.float32),
        ],
        cost_estimate=pl.CostEstimate(
            flops=16 * rows * width * BLOCK, bytes_accessed=8 * rows * width, transcendentals=0
        ),
        compiler_params=pltpu.CompilerParams(vmem_limit_bytes=VMEM_LIMIT),
    )(values, cotangent, cum_cols, cum_rows, gate_cols, skip_lanes, projected)


def outer_kernel(
    gated_ref, part_ref, weight_ref, both_ref, inner_ref, adjoint_ref, heads_ref, grads_ref
):
    state = both_ref.shape[1] // 2
    writer = both_ref[:, :state]
    adjoint = adjoint_ref[0]

    @pl.when(pl.program_id(1) == 0)
    def _():
        grads_ref[...] = inner_ref[:, :state]

    grads_ref[...] += lax.dot_general(
        gated_ref[...], adjoint, (((1,), (1,)), ((), ())), preferred_element_type=jnp.float32
    )
    weights = weight_ref[0, 0]
    for pair in range(gated_ref.shape[1] // PAIR):
        cols = slice(pair * PAIR, (pair + 1) * PAIR)
        entering = jnp.dot(writer, adjoint[:, cols], preferred_element_type=jnp.float32)
        total = part_ref[:, cols] + per_head(weights, pair) * entering
        heads_ref[:, cols] = total.astype(jnp.bfloat16)


def outer(gated, part, weight_cols, projected, inner_grads, adjoint_in):
    rows, width = gated.shape
    blocks, groups, _, heads = weight_cols.shape
    cols = width // groups
    both = projected.shape[1]
    state = both // 2
    wide = pl.BlockSpec((BLOCK, cols), lambda b, g: (b, g))
    whole = pl.BlockSpec((BLOCK, both), lambda b, g: (b, 0))
    return pl.pallas_call(
        outer_kernel,
        grid=(blocks, groups),
        in_specs=[
            wide,
            wide,
            pl.BlockSpec((1, 1, BLOCK, heads), lambda b, g: (b, g, 0, 0)),
            whole,
            whole,
            pl.BlockSpec((1, state, cols), lambda b, g: (b, 0, g)),
        ],
        out_specs=[wide, pl.BlockSpec((BLOCK, state), lambda b, g: (b, 0))],
        out_shape=[
            jax.ShapeDtypeStruct((rows, width), jnp.bfloat16),
            jax.ShapeDtypeStruct((rows, state), jnp.float32),
        ],
        cost_estimate=pl.CostEstimate(
            flops=4 * rows * width * state, bytes_accessed=8 * rows * width, transcendentals=0
        ),
        compiler_params=pltpu.CompilerParams(vmem_limit_bytes=VMEM_LIMIT),
    )(gated, part, weight_cols, projected, inner_grads, adjoint_in)


def span_logs(logs, first, last):
    index = jnp.arange(logs.shape[0])
    inside = ((index >= first) & (index < last))[:, None]
    return jnp.sum(jnp.where(inside, logs, 0.0), axis=0)


def step_logs(logs, forward):
    me = lax.axis_index("ctx")
    rows = []
    for bit in bits_of("ctx"):
        start = (me // bit) * bit
        takes = has_bit("ctx", bit) == (1 if forward else 0)
        far_first = jnp.where(takes, start, start ^ bit)
        rows.append(span_logs(logs, start, me) if forward else span_logs(logs, me + 1, start + bit))
        rows.append(span_logs(logs, far_first, far_first + bit))
    return rows


def arriving_step(carried, bit, between, passed, forward, beside):
    total, entering = carried
    got = exchange(total.astype(jnp.bfloat16), "ctx", bit)
    got, beside = lax.optimization_barrier((got, beside))
    got = got.astype(jnp.float32)
    takes = has_bit("ctx", bit) == (1 if forward else 0)
    entering = entering + jnp.where(takes, between[None] * got, 0.0)
    total = jnp.where(takes, got, total) * passed[None] + jnp.where(takes, total, got)
    return (total, entering), beside


def chain_gather(shard, axis):
    peers = lax.axis_size(axis)
    me = lax.axis_index(axis)
    rows = shard.shape[0]
    full = jnp.zeros((peers * rows,) + shard.shape[1:], shard.dtype)
    from_left = from_right = shard
    arrived = []
    for step in range(1, peers):
        from_left = lax.ppermute(from_left, axis, [(i, i + 1) for i in range(peers - 1)])
        from_right = lax.ppermute(from_right, axis, [(i, i - 1) for i in range(1, peers)])
        arrived += [(from_left, me - step), (from_right, me + step)]
    for piece, owner in arrived:
        place = jnp.where((owner >= 0) & (owner < peers), owner, me)
        full = lax.dynamic_update_slice_in_dim(full, piece, place * rows, 0)
    return lax.dynamic_update_slice_in_dim(full, shard, me * rows, 0)


def entering_blocks(terms, block_decay, arrived, forward):
    blocks = terms.shape[0]
    order = range(blocks) if forward else range(blocks - 1, -1, -1)
    held = [None] * blocks
    carried = arrived
    for block in order:
        held[block] = carried.astype(jnp.bfloat16)
        carried = block_decay[block][None, :] * carried + terms[block]
    return jnp.stack(held)


def piece_total(terms, block_decay, forward):
    blocks = terms.shape[0]
    order = range(blocks) if forward else range(blocks - 1, -1, -1)
    total = None
    for block in order:
        total = terms[block] if total is None else block_decay[block][None, :] * total + terms[block]
    return total


def product_kernel(parity_ref, left_ref, right_ref, out_ref):
    out_ref[...] = jnp.dot(
        left_ref[...], right_ref[...], preferred_element_type=jnp.float32
    ).astype(jnp.bfloat16)


def columns_product(left, right, first, width, parity):
    rows, depth = left.shape
    tile = rows // lax.axis_size("ctx")
    if width % PAIR:
        right, first = right[:, first : first + width], 0
    return pl.pallas_call(
        product_kernel,
        grid_spec=pltpu.PrefetchScalarGridSpec(
            num_scalar_prefetch=1,
            grid=(rows // (2 * tile),),
            in_specs=[
                pl.BlockSpec((tile, depth), lambda i, parity: (2 * i + parity[0], 0)),
                pl.BlockSpec((depth, width), lambda i, parity: (0, first // width)),
            ],
            out_specs=pl.BlockSpec((tile, width), lambda i, parity: (i, 0)),
        ),
        out_shape=jax.ShapeDtypeStruct((rows // 2, width), jnp.bfloat16),
        cost_estimate=pl.CostEstimate(
            flops=rows * depth * width,
            bytes_accessed=rows * depth + rows * width + 2 * depth * width,
            transcendentals=0,
        ),
        compiler_params=pltpu.CompilerParams(vmem_limit_bytes=VMEM_LIMIT),
    )(jnp.reshape(parity, (1,)).astype(jnp.int32), left, right)


def shards(layer_input, proj_weight, state_weight, out_grad, log_decay, skip_gain):
    heads = skip_gain.shape[0]
    width = out_grad.shape[1]
    head_width = width // heads
    blocks = out_grad.shape[0] // BLOCK
    state = state_weight.shape[1] // 2
    scale = state ** (-0.5)
    groups = max(1, heads // 10)
    bits = bits_of("ctx")
    high = bits[1:]

    def lanes(per_head_values):
        return jnp.repeat(per_head_values, head_width, axis=-1)

    full_weight = lax.all_gather(proj_weight, "ctx", axis=0, tiled=True)
    gathered = chain_gather(layer_input, "sp")
    half = width // 2

    shaped = log_decay.reshape(groups, heads // groups, blocks, BLOCK)
    cum_rows = jnp.cumsum(shaped, axis=3).transpose(2, 0, 1, 3)
    gate_rows = jnp.sqrt(-jnp.expm1(2.0 * shaped)).transpose(2, 0, 1, 3)
    to_end_rows = jnp.exp(cum_rows[..., -1:] - cum_rows)
    block_logs = cum_rows[..., -1].reshape(blocks, heads)
    logs = cube_gather(jnp.sum(block_logs, axis=0)[None], "ctx", bits)
    ahead, back = step_logs(logs, True), step_logs(logs, False)
    factors = lanes(jnp.exp(jnp.stack(list(block_logs) + ahead + back)))
    cum_cols = cum_rows.transpose(0, 1, 3, 2)
    gate_cols = gate_rows.transpose(0, 1, 3, 2)
    from_start_cols = jnp.exp(cum_cols)
    gate_end_cols = (gate_rows * to_end_rows).transpose(0, 1, 3, 2)

    skip_lanes = lanes(skip_gain)[None, :]
    factors, skip_lanes, cum_cols, cum_rows, gate_cols, from_start_cols, gate_end_cols, gathered = (
        lax.optimization_barrier(
            (
                factors,
                skip_lanes,
                cum_cols,
                cum_rows,
                gate_cols,
                from_start_cols,
                gate_end_cols,
                gathered,
            )
        )
    )
    block_decay = factors[:blocks]
    ahead = factors[blocks : blocks + len(ahead)]
    back = factors[blocks + len(ahead) :]

    def step(carried, number, forward, beside=()):
        rows = ahead if forward else back
        return arriving_step(
            carried, bits[number], rows[2 * number], rows[2 * number + 1], forward, beside
        )

    projected = jnp.dot(gathered, state_weight, preferred_element_type=jnp.float32).astype(
        jnp.bfloat16
    )
    turned = projected.reshape(blocks, BLOCK, 2 * state).transpose(0, 2, 1)
    scaled_cot, pending = weigh(out_grad, from_start_cols, turned[:, state:])
    pending = pending * scale
    total = piece_total(pending, block_decay, False)
    adjoint, _ = step((total, jnp.zeros_like(total)), 0, False)
    adjoint, gathered = lax.optimization_barrier((adjoint, gathered))
    values = jnp.dot(gathered, full_weight, preferred_element_type=jnp.float32).astype(jnp.bfloat16)
    adjoint, values = step(adjoint, 1, False, values)
    gated, written = weigh(values, gate_end_cols, turned[:, :state])
    total = piece_total(written, block_decay, True)
    arriving, _ = step((total, jnp.zeros_like(total)), 0, True)
    adjoint, arriving, values = lax.optimization_barrier((adjoint, arriving, values))
    part, inner_grads = inner(
        values, out_grad, cum_cols, cum_rows, gate_cols, skip_lanes, projected
    )
    for number in range(2, len(bits)):
        adjoint, part = step(adjoint, number, False, part)
    for number in range(1, len(bits) - 1):
        arriving, part = step(arriving, number, True, part)
    adjoint_in = entering_blocks(pending, block_decay, adjoint[1], False)
    turned_input, part = lax.optimization_barrier((gathered.T, part))
    grad_heads, grad_writer = outer(
        gated, part, gate_end_cols, projected, inner_grads, adjoint_in
    )
    own = has_bit("ctx", bits[0])
    sends = [
        columns_product(turned_input, grad_heads, first, half, 1 - own) for first in (0, half)
    ]
    arriving, (sends, grad_heads) = step(arriving, len(bits) - 1, True, (sends, grad_heads))
    state_in = entering_blocks(written, block_decay, arriving[1], True)

    across = (((1,), (1,)), ((), ()))
    dot = functools.partial(lax.dot_general, preferred_element_type=jnp.float32)
    read = jnp.einsum(
        "bsw,bnw->bsn",
        scaled_cot.reshape(blocks, BLOCK, width),
        state_in,
        preferred_element_type=jnp.float32,
    ).reshape(-1, state)
    grad_reader = inner_grads[:, state:] + scale * read
    low_grads = jnp.concatenate([grad_writer, grad_reader], axis=1).astype(jnp.bfloat16)
    input_terms = (
        dot(grad_heads, full_weight, across) + dot(low_grads, state_weight, across)
    ).astype(jnp.bfloat16)
    input_terms, turned_input, grad_heads, low_grads = lax.optimization_barrier(
        (input_terms, turned_input, grad_heads, low_grads)
    )
    grad_input = lax.psum_scatter(input_terms, "sp", scatter_dimension=0, tiled=True)
    grad_scale = (gathered.shape[0] * lax.axis_size("ctx")) ** (-0.5)
    high = bits[1:]
    low_send = columns_product(turned_input, low_grads, 0, 2 * state, 1 - own)
    keeps = [columns_product(turned_input, grad_heads, first, half, own) for first in (0, half)]
    low_keep = columns_product(turned_input, low_grads, 0, 2 * state, own)
    sum_a = cube_scatter(keeps[0], sends[0], "ctx", high)
    sum_b = cube_scatter(keeps[1], sends[1], "ctx", high[::-1])
    sum_s = cube_scatter(low_keep, low_send, "ctx", high)
    grad_proj = jnp.concatenate([sum_a, sum_b], axis=1) * grad_scale
    low = sum_s.astype(jnp.bfloat16).reshape(-1, 2, sum_s.shape[0] // lax.axis_size("sp"), 2 * state)
    pick = has_bit("sp", 1)
    keep, send = (
        lax.dynamic_index_in_dim(low, bit, 1, False).reshape(-1, 2 * state)
        for bit in (pick, 1 - pick)
    )
    grad_state = cube_scatter(keep, send, "sp", bits_of("sp")[1:]) * grad_scale
    return (grad_input, grad_proj, grad_state)


def solution(mesh):
    in_specs = (
        P(("ctx", "sp"), None),
        P("ctx", "sp"),
        P(),
        P("ctx", "sp"),
        P("sp", "ctx"),
        P("sp"),
    )
    out_specs = (P(("ctx", "sp"), None), P("ctx", "sp"), P(("ctx", "sp"), None))
    return jax.shard_map(shards, mesh=mesh, in_specs=in_specs, out_specs=out_specs, check_vma=False)
```

```python
import functools

import jax
import jax.numpy as jnp
from jax import lax
from jax.experimental import pallas as pl
from jax.experimental.pallas import tpu as pltpu
from jax.sharding import PartitionSpec as P

BLOCK = 256
PAIR = 128
VMEM_LIMIT = 48 * 1024 * 1024


def exchange(array, axis, bit):
    peers = lax.axis_size(axis)
    return lax.ppermute(array, axis, [(i, i ^ bit) for i in range(peers)])


def bits_of(axis):
    peers = lax.axis_size(axis)
    return [1 << k for k in range(peers.bit_length() - 1)]


def has_bit(axis, bit):
    return (lax.axis_index(axis) // bit) % 2


def cube_gather(shard, axis, order):
    bits = bits_of(axis)
    array = shard.reshape((1,) * len(bits) + shard.shape)
    for bit in order:
        dim = len(bits) - bit.bit_length()
        other = exchange(array, axis, bit)
        upper = has_bit(axis, bit) == 1
        array = jnp.concatenate(
            [jnp.where(upper, other, array), jnp.where(upper, array, other)], axis=dim
        )
    return array.reshape((-1,) + shard.shape[1:])


def cube_scatter(keep, got, axis, order):
    bits = bits_of(axis)
    rows = 2 * keep.shape[0] // lax.axis_size(axis)
    total = keep.astype(jnp.float32) + got.astype(jnp.float32)
    total = total.reshape((2,) * (len(bits) - 1) + (rows,) + keep.shape[1:])
    for bit in order:
        dim = len(bits) - bit.bit_length()
        own = has_bit(axis, bit)
        array = total.astype(jnp.bfloat16)
        keep = lax.dynamic_slice_in_dim(array, own, 1, dim)
        send = lax.dynamic_slice_in_dim(array, 1 - own, 1, dim)
        got = exchange(send, axis, bit)
        total = keep.astype(jnp.float32) + got.astype(jnp.float32)
    return total.reshape((rows,) + total.shape[len(bits) :])


def per_head(columns, pair):
    low = jnp.broadcast_to(columns[:, 2 * pair : 2 * pair + 1], (columns.shape[0], PAIR // 2))
    high = jnp.broadcast_to(columns[:, 2 * pair + 1 : 2 * pair + 2], (columns.shape[0], PAIR // 2))
    return jnp.concatenate([low, high], axis=1)


def weigh_kernel(x_ref, weight_ref, left_ref, weighted_ref, out_ref):
    weights = weight_ref[0, 0]
    for pair in range(x_ref.shape[1] // PAIR):
        cols = slice(pair * PAIR, (pair + 1) * PAIR)
        scaled = (x_ref[:, cols].astype(jnp.float32) * per_head(weights, pair)).astype(jnp.bfloat16)
        weighted_ref[:, cols] = scaled
        out_ref[0, :, cols] = jnp.dot(left_ref[0], scaled, preferred_element_type=jnp.float32)


def weigh(x, weights, left):
    rows, width = x.shape
    blocks, groups, _, heads = weights.shape
    cols = width // groups
    state = left.shape[1]
    return pl.pallas_call(
        weigh_kernel,
        grid=(blocks, groups),
        in_specs=[
            pl.BlockSpec((BLOCK, cols), lambda b, g: (b, g)),
            pl.BlockSpec((1, 1, BLOCK, heads), lambda b, g: (b, g, 0, 0)),
            pl.BlockSpec((1, state, BLOCK), lambda b, g: (b, 0, 0)),
        ],
        out_specs=[
            pl.BlockSpec((BLOCK, cols), lambda b, g: (b, g)),
            pl.BlockSpec((1, state, cols), lambda b, g: (b, 0, g)),
        ],
        out_shape=[
            jax.ShapeDtypeStruct((rows, width), jnp.bfloat16),
            jax.ShapeDtypeStruct((blocks, state, width), jnp.float32),
        ],
        cost_estimate=pl.CostEstimate(
            flops=2 * rows * width * state, bytes_accessed=6 * rows * width, transcendentals=0
        ),
        compiler_params=pltpu.CompilerParams(vmem_limit_bytes=VMEM_LIMIT),
    )(x, weights, left)


def inner_kernel(
    scale, x_ref, c_ref, cumc_ref, cumr_ref, gate_ref, skip_ref, both_ref,
    part_ref, grads_ref, mix_ref, sum_ref,
):
    group = pl.program_id(1)
    state = both_ref.shape[1] // 2
    writer = both_ref[:, :state]
    reader = both_ref[:, state:]
    cross = (((1,), (1,)), ((), ()))

    @pl.when(group == 0)
    def _():
        mix_ref[...] = lax.dot_general(
            writer, reader, cross, preferred_element_type=jnp.float32
        )
        sum_ref[...] = jnp.zeros_like(sum_ref)

    source = lax.broadcasted_iota(jnp.int32, (BLOCK, BLOCK), 0)
    target = lax.broadcasted_iota(jnp.int32, (BLOCK, BLOCK), 1)
    causal = target >= source
    half = PAIR // 2
    for pair in range(x_ref.shape[1] // PAIR):
        carried = []
        for side in range(2):
            head = 2 * pair + side
            cols = slice(head * half, (head + 1) * half)
            cot = c_ref[:, cols]
            exponent = cumr_ref[0, 0, head : head + 1, :] - cumc_ref[0, 0, :, head : head + 1]
            decays = jnp.exp(jnp.where(causal, exponent, -1e30))
            gram = lax.dot_general(x_ref[:, cols], cot, cross, preferred_element_type=jnp.float32)
            gate = gate_ref[0, 0, :, head : head + 1]
            sum_ref[...] += (decays * gram) * gate
            mixing = (decays * mix_ref[...]).astype(jnp.bfloat16)
            carried.append(
                jnp.dot(mixing, cot, preferred_element_type=jnp.float32) * (gate * scale)
            )
        cols = slice(pair * PAIR, (pair + 1) * PAIR)
        part_ref[:, cols] = jnp.concatenate(carried, axis=1) + skip_ref[:, cols] * c_ref[
            :, cols
        ].astype(jnp.float32)

    @pl.when(group == pl.num_programs(1) - 1)
    def _():
        low = sum_ref[...].astype(jnp.bfloat16)
        grads_ref[:, :state] = scale * jnp.dot(low, reader, preferred_element_type=jnp.float32)
        grads_ref[:, state:] = scale * lax.dot_general(
            low, writer, (((0,), (0,)), ((), ())), preferred_element_type=jnp.float32
        )


def inner(values, cotangent, cum_cols, cum_rows, gate_cols, skip_lanes, projected):
    rows, width = values.shape
    blocks, groups, _, heads = cum_cols.shape
    cols = width // groups
    both = projected.shape[1]
    scale = (both // 2) ** (-0.5)
    column_spec = pl.BlockSpec((1, 1, BLOCK, heads), lambda b, g: (b, g, 0, 0))
    wide = pl.BlockSpec((BLOCK, cols), lambda b, g: (b, g))
    whole = pl.BlockSpec((BLOCK, both), lambda b, g: (b, 0))
    return pl.pallas_call(
        lambda x, c, cc, cr, gt, sk, bo, part, grads, mix, total: inner_kernel(
            scale, x, c, cc, cr, gt, sk, bo, part, grads, mix, total
        ),
        grid=(blocks, groups),
        in_specs=[
            wide,
            wide,
            column_spec,
            pl.BlockSpec((1, 1, heads, BLOCK), lambda b, g: (b, g, 0, 0)),
            column_spec,
            pl.BlockSpec((1, cols), lambda b, g: (0, g)),
            whole,
        ],
        out_specs=[wide, whole],
        out_shape=[
            jax.ShapeDtypeStruct((rows, width), jnp.float32),
            jax.ShapeDtypeStruct((rows, both), jnp.float32),
        ],
        scratch_shapes=[
            pltpu.VMEM((BLOCK, BLOCK), jnp.float32),
            pltpu.VMEM((BLOCK, BLOCK), jnp.float32),
        ],
        cost_estimate=pl.CostEstimate(
            flops=16 * rows * width * BLOCK, bytes_accessed=8 * rows * width, transcendentals=0
        ),
        compiler_params=pltpu.CompilerParams(vmem_limit_bytes=VMEM_LIMIT),
    )(values, cotangent, cum_cols, cum_rows, gate_cols, skip_lanes, projected)


def outer_kernel(
    gated_ref, part_ref, weight_ref, both_ref, inner_ref, adjoint_ref, heads_ref, grads_ref
):
    state = both_ref.shape[1] // 2
    writer = both_ref[:, :state]
    adjoint = adjoint_ref[0]

    @pl.when(pl.program_id(1) == 0)
    def _():
        grads_ref[...] = inner_ref[:, :state]

    grads_ref[...] += lax.dot_general(
        gated_ref[...], adjoint, (((1,), (1,)), ((), ())), preferred_element_type=jnp.float32
    )
    weights = weight_ref[0, 0]
    for pair in range(gated_ref.shape[1] // PAIR):
        cols = slice(pair * PAIR, (pair + 1) * PAIR)
        entering = jnp.dot(writer, adjoint[:, cols], preferred_element_type=jnp.float32)
        total = part_ref[:, cols] + per_head(weights, pair) * entering
        heads_ref[:, cols] = total.astype(jnp.bfloat16)


def outer(gated, part, weight_cols, projected, inner_grads, adjoint_in):
    rows, width = gated.shape
    blocks, groups, _, heads = weight_cols.shape
    cols = width // groups
    both = projected.shape[1]
    state = both // 2
    wide = pl.BlockSpec((BLOCK, cols), lambda b, g: (b, g))
    whole = pl.BlockSpec((BLOCK, both), lambda b, g: (b, 0))
    return pl.pallas_call(
        outer_kernel,
        grid=(blocks, groups),
        in_specs=[
            wide,
            wide,
            pl.BlockSpec((1, 1, BLOCK, heads), lambda b, g: (b, g, 0, 0)),
            whole,
            whole,
            pl.BlockSpec((1, state, cols), lambda b, g: (b, 0, g)),
        ],
        out_specs=[wide, pl.BlockSpec((BLOCK, state), lambda b, g: (b, 0))],
        out_shape=[
            jax.ShapeDtypeStruct((rows, width), jnp.bfloat16),
            jax.ShapeDtypeStruct((rows, state), jnp.float32),
        ],
        cost_estimate=pl.CostEstimate(
            flops=4 * rows * width * state, bytes_accessed=8 * rows * width, transcendentals=0
        ),
        compiler_params=pltpu.CompilerParams(vmem_limit_bytes=VMEM_LIMIT),
    )(gated, part, weight_cols, projected, inner_grads, adjoint_in)


def span_logs(logs, first, last):
    index = jnp.arange(logs.shape[0])
    inside = ((index >= first) & (index < last))[:, None]
    return jnp.sum(jnp.where(inside, logs, 0.0), axis=0)


def step_logs(logs, forward):
    me = lax.axis_index("ctx")
    rows = []
    for bit in bits_of("ctx"):
        start = (me // bit) * bit
        takes = has_bit("ctx", bit) == (1 if forward else 0)
        far_first = jnp.where(takes, start, start ^ bit)
        rows.append(span_logs(logs, start, me) if forward else span_logs(logs, me + 1, start + bit))
        rows.append(span_logs(logs, far_first, far_first + bit))
    return rows


def arriving_step(carried, bit, between, passed, forward, beside):
    total, entering = carried
    got = exchange(total.astype(jnp.bfloat16), "ctx", bit)
    got, beside = lax.optimization_barrier((got, beside))
    got = got.astype(jnp.float32)
    takes = has_bit("ctx", bit) == (1 if forward else 0)
    entering = entering + jnp.where(takes, between[None] * got, 0.0)
    total = jnp.where(takes, got, total) * passed[None] + jnp.where(takes, total, got)
    return (total, entering), beside


def chain_gather(shard, axis):
    peers = lax.axis_size(axis)
    me = lax.axis_index(axis)
    rows = shard.shape[0]
    full = jnp.zeros((peers * rows,) + shard.shape[1:], shard.dtype)
    from_left = from_right = shard
    arrived = []
    for step in range(1, peers):
        from_left = lax.ppermute(from_left, axis, [(i, i + 1) for i in range(peers - 1)])
        from_right = lax.ppermute(from_right, axis, [(i, i - 1) for i in range(1, peers)])
        arrived += [(from_left, me - step), (from_right, me + step)]
    for piece, owner in arrived:
        place = jnp.where((owner >= 0) & (owner < peers), owner, me)
        full = lax.dynamic_update_slice_in_dim(full, piece, place * rows, 0)
    return lax.dynamic_update_slice_in_dim(full, shard, me * rows, 0)


def entering_blocks(terms, block_decay, arrived, forward):
    blocks = terms.shape[0]
    order = range(blocks) if forward else range(blocks - 1, -1, -1)
    held = [None] * blocks
    carried = arrived
    for block in order:
        held[block] = carried.astype(jnp.bfloat16)
        carried = block_decay[block][None, :] * carried + terms[block]
    return jnp.stack(held)


def piece_total(terms, block_decay, forward):
    blocks = terms.shape[0]
    order = range(blocks) if forward else range(blocks - 1, -1, -1)
    total = None
    for block in order:
        total = terms[block] if total is None else block_decay[block][None, :] * total + terms[block]
    return total


def product_kernel(parity_ref, left_ref, right_ref, out_ref):
    out_ref[...] = jnp.dot(
        left_ref[...], right_ref[...], preferred_element_type=jnp.float32
    ).astype(jnp.bfloat16)


def columns_product(left, right, first, width, parity):
    rows, depth = left.shape
    tile = rows // lax.axis_size("ctx")
    if width % PAIR:
        right, first = right[:, first : first + width], 0
    return pl.pallas_call(
        product_kernel,
        grid_spec=pltpu.PrefetchScalarGridSpec(
            num_scalar_prefetch=1,
            grid=(rows // (2 * tile),),
            in_specs=[
                pl.BlockSpec((tile, depth), lambda i, parity: (2 * i + parity[0], 0)),
                pl.BlockSpec((depth, width), lambda i, parity: (0, first // width)),
            ],
            out_specs=pl.BlockSpec((tile, width), lambda i, parity: (i, 0)),
        ),
        out_shape=jax.ShapeDtypeStruct((rows // 2, width), jnp.bfloat16),
        cost_estimate=pl.CostEstimate(
            flops=rows * depth * width,
            bytes_accessed=rows * depth + rows * width + 2 * depth * width,
            transcendentals=0,
        ),
        compiler_params=pltpu.CompilerParams(vmem_limit_bytes=VMEM_LIMIT),
    )(jnp.reshape(parity, (1,)).astype(jnp.int32), left, right)


def shards(layer_input, proj_weight, state_weight, out_grad, log_decay, skip_gain):
    heads = skip_gain.shape[0]
    width = out_grad.shape[1]
    head_width = width // heads
    blocks = out_grad.shape[0] // BLOCK
    state = state_weight.shape[1] // 2
    scale = state ** (-0.5)
    groups = max(1, heads // 10)
    bits = bits_of("ctx")
    high = bits[1:]

    def lanes(per_head_values):
        return jnp.repeat(per_head_values, head_width, axis=-1)

    full_weight = lax.all_gather(proj_weight, "ctx", axis=0, tiled=True)
    gathered = chain_gather(layer_input, "sp")
    half = width // 2

    shaped = log_decay.reshape(groups, heads // groups, blocks, BLOCK)
    cum_rows = jnp.cumsum(shaped, axis=3).transpose(2, 0, 1, 3)
    gate_rows = jnp.sqrt(-jnp.expm1(2.0 * shaped)).transpose(2, 0, 1, 3)
    to_end_rows = jnp.exp(cum_rows[..., -1:] - cum_rows)
    block_logs = cum_rows[..., -1].reshape(blocks, heads)
    logs = cube_gather(jnp.sum(block_logs, axis=0)[None], "ctx", bits)
    ahead, back = step_logs(logs, True), step_logs(logs, False)
    factors = lanes(jnp.exp(jnp.stack(list(block_logs) + ahead + back)))
    cum_cols = cum_rows.transpose(0, 1, 3, 2)
    gate_cols = gate_rows.transpose(0, 1, 3, 2)
    from_start_cols = jnp.exp(cum_cols)
    gate_end_cols = (gate_rows * to_end_rows).transpose(0, 1, 3, 2)

    skip_lanes = lanes(skip_gain)[None, :]
    factors, skip_lanes, cum_cols, cum_rows, gate_cols, from_start_cols, gate_end_cols, gathered = (
        lax.optimization_barrier(
            (
                factors,
                skip_lanes,
                cum_cols,
                cum_rows,
                gate_cols,
                from_start_cols,
                gate_end_cols,
                gathered,
            )
        )
    )
    block_decay = factors[:blocks]
    ahead = factors[blocks : blocks + len(ahead)]
    back = factors[blocks + len(ahead) :]

    def step(carried, number, forward, beside=()):
        rows = ahead if forward else back
        return arriving_step(
            carried, bits[number], rows[2 * number], rows[2 * number + 1], forward, beside
        )

    projected = jnp.dot(gathered, state_weight, preferred_element_type=jnp.float32).astype(
        jnp.bfloat16
    )
    turned = projected.reshape(blocks, BLOCK, 2 * state).transpose(0, 2, 1)
    scaled_cot, pending = weigh(out_grad, from_start_cols, turned[:, state:])
    pending = pending * scale
    total = piece_total(pending, block_decay, False)
    adjoint, _ = step((total, jnp.zeros_like(total)), 0, False)
    adjoint, gathered = lax.optimization_barrier((adjoint, gathered))
    values = jnp.dot(gathered, full_weight, preferred_element_type=jnp.float32).astype(jnp.bfloat16)
    adjoint, values = step(adjoint, 1, False, values)
    gated, written = weigh(values, gate_end_cols, turned[:, :state])
    total = piece_total(written, block_decay, True)
    arriving, _ = step((total, jnp.zeros_like(total)), 0, True)
    adjoint, arriving, values = lax.optimization_barrier((adjoint, arriving, values))
    part, inner_grads = inner(
        values, out_grad, cum_cols, cum_rows, gate_cols, skip_lanes, projected
    )
    for number in range(2, len(bits)):
        adjoint, part = step(adjoint, number, False, part)
    for number in range(1, len(bits) - 1):
        arriving, part = step(arriving, number, True, part)
    adjoint_in = entering_blocks(pending, block_decay, adjoint[1], False)
    turned_input, part = lax.optimization_barrier((gathered.T, part))
    grad_heads, grad_writer = outer(
        gated, part, gate_end_cols, projected, inner_grads, adjoint_in
    )
    own = has_bit("ctx", bits[0])
    sends = [
        columns_product(turned_input, grad_heads, first, half, 1 - own) for first in (0, half)
    ]
    sends, grad_heads = lax.optimization_barrier((sends, grad_heads))
    moved = [exchange(send, "ctx", bits[0]) for send in sends]
    arriving, grad_heads = step(arriving, len(bits) - 1, True, grad_heads)
    state_in = entering_blocks(written, block_decay, arriving[1], True)

    across = (((1,), (1,)), ((), ()))
    dot = functools.partial(lax.dot_general, preferred_element_type=jnp.float32)
    read = jnp.einsum(
        "bsw,bnw->bsn",
        scaled_cot.reshape(blocks, BLOCK, width),
        state_in,
        preferred_element_type=jnp.float32,
    ).reshape(-1, state)
    grad_reader = inner_grads[:, state:] + scale * read
    low_grads = jnp.concatenate([grad_writer, grad_reader], axis=1).astype(jnp.bfloat16)
    input_terms = (
        dot(grad_heads, full_weight, across) + dot(low_grads, state_weight, across)
    ).astype(jnp.bfloat16)
    input_terms, turned_input, grad_heads, low_grads = lax.optimization_barrier(
        (input_terms, turned_input, grad_heads, low_grads)
    )
    grad_input = lax.psum_scatter(input_terms, "sp", scatter_dimension=0, tiled=True)
    grad_scale = (gathered.shape[0] * lax.axis_size("ctx")) ** (-0.5)
    high = bits[1:]
    moved, low_grads = lax.optimization_barrier((moved, low_grads))
    low_send = columns_product(turned_input, low_grads, 0, 2 * state, 1 - own)
    keeps = [columns_product(turned_input, grad_heads, first, half, own) for first in (0, half)]
    low_keep = columns_product(turned_input, low_grads, 0, 2 * state, own)
    sum_a = cube_scatter(keeps[0], moved[0], "ctx", high)
    sum_b = cube_scatter(keeps[1], moved[1], "ctx", high[::-1])
    sum_s = cube_scatter(low_keep, exchange(low_send, "ctx", bits[0]), "ctx", high)
    grad_proj = jnp.concatenate([sum_a, sum_b], axis=1) * grad_scale
    low = sum_s.astype(jnp.bfloat16).reshape(-1, 2, sum_s.shape[0] // lax.axis_size("sp"), 2 * state)
    pick = has_bit("sp", 1)
    keep, send = (
        lax.dynamic_index_in_dim(low, bit, 1, False).reshape(-1, 2 * state)
        for bit in (pick, 1 - pick)
    )
    grad_state = cube_scatter(keep, exchange(send, "sp", 1), "sp", bits_of("sp")[1:]) * grad_scale
    return (grad_input, grad_proj, grad_state)


def solution(mesh):
    in_specs = (
        P(("ctx", "sp"), None),
        P("ctx", "sp"),
        P(),
        P("ctx", "sp"),
        P("sp", "ctx"),
        P("sp"),
    )
    out_specs = (P(("ctx", "sp"), None), P("ctx", "sp"), P(("ctx", "sp"), None))
    return jax.shard_map(shards, mesh=mesh, in_specs=in_specs, out_specs=out_specs, check_vma=False)
```
